256 devices in a mesh: section: 2 (over core), row: 16 (over y, x), col: 8 (over z).
Axes of the slice: x: 4, y: 4, z: 8, core: 2. Of those that a mesh axis runs over, the one named last changes fastest.
Arguments:
- tables: bfloat16 [32, 4096, 256], P('col', ('section', 'row')), may hold values from -1.5 to 1.5
- bag_index: int32 [1024, 32, 32], P(None, 'col'), may hold values from 0 to 4096, as said below
- cross_weight: bfloat16 [2, 8192, 8192], P(None, 'col', ('section', 'row')), may hold values from -0.0625 to 0.0625
- cross_bias: float32 [2, 8192], replicated, may hold values from -3 to 3
- upstream: bfloat16 [1024, 8192], P(('section', 'row'), 'col'), may hold values from -6 to 6
Outputs:
- crossed: bfloat16 [1024, 8192], P(('section', 'row'), 'col')
- pooled_grad: float32 [1024, 8192], P(('section', 'row'), 'col')
- table_grad: float32 [32, 4096, 256], P('col', ('section', 'row'))
- weight_grad: float32 [2, 8192, 8192], P(None, 'col', ('section', 'row'))
- bias_grad: float32 [2, 8192], P(None, ('section', 'row'))
The draws below stay inside these ranges and needn't reach their ends.
Inputs may be any that keep to these rules, and one draw needn't show every extreme that they name: `bag_index`: each bag lists 1 to 32 table rows first, then only the padding value 4096, which stands for a zero row.
All inputs are finite; a program needn't handle non-finite values.
Results may differ from the reference program's by a relative error of at most 0.012.
Values may be sent and summed in bfloat16 or wider, within the bound.
No kernel may reach another device: no remote copies, remote signals or barrier semaphores. Data moves between devices by JAX's collectives and lax.ppermute only.
A program may use at most 64 MiB of HBM per device.

```python
import jax
import jax.numpy as jnp
from jax import lax

F = 32
E = 256
BAG = 32
LAYERS = 2
D = 8192
BATCH = 1024
VOCAB = 4096


def draw_bag_index(key, part):
    base_key = jax.random.fold_in(key, 11)
    length_key, row_key = jax.random.split(base_key)
    lengths = jax.random.randint(length_key, (BATCH, F, 1), 1, BAG + 1)
    row_ids = jax.random.randint(row_key, (BATCH, F, BAG), 0, VOCAB)
    positions = lax.broadcasted_iota(jnp.int32, (BATCH, F, BAG), 2)
    return jnp.where(positions < lengths, row_ids, VOCAB).astype(jnp.int32)


def steps_of(stream_key, extent, cuts, least, high):
    def one(axis_at, parts):
        heights = jax.random.uniform(jax.random.fold_in(jax.random.fold_in(stream_key, 6), axis_at), (parts,), jnp.float32, least / len(cuts), high / len(cuts))
        return jnp.repeat(jnp.exp(heights), extent[axis_at] // parts).reshape((-1,) + (1,) * (len(extent) - axis_at - 1))

    loudness = one(*cuts[0])
    for cut in cuts[1:]:
        loudness = loudness * one(*cut)
    return loudness


def normal_values(stream_key, shape, width, reach, pieces=(), kind=jnp.bfloat16):
    drawn = width * jax.random.normal(stream_key, shape, jnp.float32)
    if pieces:
        drawn = drawn * steps_of(stream_key, shape, pieces, -0.22, 0.18)
    return jnp.clip(drawn, -reach, reach).astype(kind)


def setup_inputs(seed: int = 0) -> dict:
    key_of = jax.random.split(jax.random.key(seed), 6)
    tables = normal_values(key_of[0], (F, VOCAB, E), 0.25, 1.5, ((0, 8), (1, 32)))
    bag_index = draw_bag_index(jax.random.fold_in(key_of[5], 71), 0)
    cross_weight = normal_values(key_of[2], (LAYERS, D, D), D ** -0.5, 0.0625, ((1, 8), (2, 32)))
    cross_bias = normal_values(key_of[3], (LAYERS, D), 0.5, 3.0, (), jnp.float32)
    upstream = normal_values(key_of[4], (BATCH, D), 1.0, 6.0, ((0, 32), (1, 8)))
    return {"tables": tables, "bag_index": bag_index, "cross_weight": cross_weight, "cross_bias": cross_bias, "upstream": upstream}


def pool_feature(operands):
    table_rows, bag_rows = operands
    padded = jnp.concatenate([table_rows, jnp.zeros((1, table_rows.shape[1]), table_rows.dtype)], axis=0)
    picked = jnp.take(padded, bag_rows, axis=0)
    return jnp.sum(picked.astype(jnp.float32), axis=1)


def spread_feature(operands):
    bag_rows, grad_rows = operands
    values = jnp.broadcast_to(grad_rows[:, None, :], (BATCH, BAG, E)).reshape(BATCH * BAG, E)
    summed = jax.ops.segment_sum(values, bag_rows.reshape(-1), num_segments=VOCAB + 1)
    return summed[:VOCAB]


def reference(tables, bag_index, cross_weight, cross_bias, upstream):
    index_major = jnp.transpose(bag_index, (1, 0, 2))
    pooled_parts = lax.map(pool_feature, (tables, index_major))
    pooled = jnp.transpose(pooled_parts, (1, 0, 2)).reshape(BATCH, D).astype(jnp.bfloat16)
    pooled_wide = pooled.astype(jnp.float32)
    current = pooled
    inputs = []
    outputs = []
    for layer_at in range(LAYERS):
        mixed_out = jnp.dot(current, cross_weight[layer_at], preferred_element_type=jnp.float32) + cross_bias[layer_at]
        inputs.append(current)
        outputs.append(mixed_out)
        current = (pooled_wide * mixed_out + current.astype(jnp.float32)).astype(jnp.bfloat16)
    crossed = current
    gradient = upstream.astype(jnp.float32)
    carried = jnp.zeros((BATCH, D), jnp.float32)
    weight_grads = [None] * LAYERS
    bias_grads = [None] * LAYERS
    for layer_at in reversed(range(LAYERS)):
        delta_rows = (pooled_wide * gradient).astype(jnp.bfloat16)
        weight_grads[layer_at] = jnp.dot(inputs[layer_at].T, delta_rows, preferred_element_type=jnp.float32)
        bias_grads[layer_at] = jnp.sum(delta_rows.astype(jnp.float32), axis=0)
        carried = carried + gradient * outputs[layer_at]
        gradient = gradient + jnp.dot(delta_rows, cross_weight[layer_at].T, preferred_element_type=jnp.float32)
    pooled_grad = gradient + carried
    rounded = lax.optimization_barrier(pooled_grad.astype(jnp.bfloat16)).astype(jnp.float32)
    per_feature = jnp.transpose(rounded.reshape(BATCH, F, E), (1, 0, 2))
    table_grad = lax.map(spread_feature, (index_major, per_feature))
    return crossed, pooled_grad, table_grad, jnp.stack(weight_grads), jnp.stack(bias_grads)
```

```python
import functools

import jax
import jax.numpy as jnp
from jax import lax
from jax.experimental import pallas as pl
from jax.experimental.pallas import tpu as pltpu
from jax.sharding import Mesh, PartitionSpec as P

NS, NY, NX, NZ = 2, 4, 4, 8
ALL = ("s", "y", "x", "z")
PLANE = ("x", "y")
BF = jnp.bfloat16
F32 = jnp.float32
VMEM_LIMIT = 40 * 1024 * 1024


def device_number(s, y, x, z):
    return ((s * NY + y) * NX + x) * NZ + z


def pairs_of(target):
    found = []
    for s in range(NS):
        for y in range(NY):
            for x in range(NX):
                for z in range(NZ):
                    found.append((device_number(s, y, x, z), device_number(*target(s, y, x, z))))
    return found


def u_to_t(value):
    return lax.ppermute(
        value, ALL, pairs_of(lambda s, y, x, z: (s, z % NY, x, 2 * y + ((z // NY) ^ s)))
    )


def t_to_u(value):
    return lax.ppermute(
        value, ALL, pairs_of(lambda s, y, x, z: (s, z // 2, x, ((z % 2) ^ s) * NY + y))
    )


def other_core(value):
    return lax.ppermute(value, "s", [(0, 1), (1, 0)])


def scatter_plane(pieces):
    arrived = lax.all_to_all(pieces, PLANE, 0, 0, tiled=True)
    return jnp.sum(arrived.astype(F32), axis=0)


def gather_plane(piece):
    spread = jnp.broadcast_to(piece[None], (NX * NY,) + piece.shape)
    return lax.all_to_all(spread, PLANE, 0, 0, tiled=True)


def scatter_depth(pieces):
    arrived = lax.all_to_all(pieces, "z", 0, 0, tiled=True)
    return jnp.sum(arrived.astype(F32), axis=0)


def gather_depth(piece):
    spread = jnp.broadcast_to(piece[None], (NZ,) + piece.shape)
    return lax.all_to_all(spread, "z", 0, 0, tiled=True)


def params():
    return pltpu.CompilerParams(vmem_limit_bytes=VMEM_LIMIT)


def pool_kernel(ids_ref, own_ref, other_ref, counts_ref, pooled_ref):
    bag_len, rows = ids_ref.shape[1:]
    slots = counts_ref.shape[1]
    lanes = 128
    for first in range(0, rows, lanes):
        slot_ids = lax.broadcasted_iota(jnp.int32, (slots, lanes), 0).astype(F32).astype(BF)
        total = jnp.zeros((slots, lanes), BF)
        for position in range(bag_len):
            wanted = ids_ref[0, position : position + 1, first : first + lanes]
            wanted = jnp.broadcast_to(wanted, (slots, lanes)).astype(BF)
            total = total + jnp.where(wanted == slot_ids, jnp.ones((), BF), jnp.zeros((), BF))
        counts_ref[0, :, first : first + lanes] = total
    half = slots // 2
    dims = (((0,), (0,)), ((), ()))
    summed = lax.dot_general(counts_ref[0, :half, :], own_ref[0], dims, preferred_element_type=F32)
    summed += lax.dot_general(counts_ref[0, half:, :], other_ref[0], dims, preferred_element_type=F32)
    pooled_ref[0] = summed.astype(BF)


def pool(ids, own_table, other_table):
    feats, bag_len, rows = ids.shape
    _, shard, width = own_table.shape
    one = lambda f: (f, 0, 0)
    return pl.pallas_call(
        pool_kernel,
        grid=(feats,),
        in_specs=[
            pl.BlockSpec((1, bag_len, rows), one),
            pl.BlockSpec((1, shard, width), one),
            pl.BlockSpec((1, shard, width), one),
        ],
        out_specs=[
            pl.BlockSpec((1, 2 * shard, rows), one),
            pl.BlockSpec((1, rows, width), one),
        ],
        out_shape=[
            jax.ShapeDtypeStruct((feats, 2 * shard, rows), BF),
            jax.ShapeDtypeStruct((feats, rows, width), BF),
        ],
        compiler_params=params(),
        name="pool",
    )(ids, own_table, other_table)


def forward_kernel(x_ref, own_ref, other_ref, out_ref):
    parts, rows, width = x_ref.shape
    piece = rows // NY
    for u, w_ref in enumerate((own_ref, other_ref)):
        total = jnp.dot(x_ref[0], w_ref[0:width, :], preferred_element_type=F32)
        for part in range(1, parts):
            total += jnp.dot(
                x_ref[part], w_ref[part * width : (part + 1) * width, :], preferred_element_type=F32
            )
        total = total.astype(BF)
        for y in range(NY):
            out_ref[2 * y + u] = total[y * piece : (y + 1) * piece]


def forward_product(x_full, own_weight, other_weight):
    parts, rows, width = x_full.shape
    return pl.pallas_call(
        forward_kernel,
        out_shape=jax.ShapeDtypeStruct((NZ, rows // NY, own_weight.shape[1]), BF),
        compiler_params=params(),
        name="forward_product",
    )(x_full, own_weight, other_weight)


def rows_of(d_ref, u):
    return jnp.concatenate([d_ref[2 * y + u] for y in range(NY)], axis=0)


def backward_kernel(d_ref, own_ref, other_ref, out_ref):
    parts, rows, width = out_ref.shape
    dims = (((1,), (1,)), ((), ()))
    own_d, other_d = rows_of(d_ref, 0), rows_of(d_ref, 1)
    for part in range(parts):
        span = slice(part * width, (part + 1) * width)
        total = lax.dot_general(own_d, own_ref[span, :], dims, preferred_element_type=F32)
        total += lax.dot_general(other_d, other_ref[span, :], dims, preferred_element_type=F32)
        out_ref[part] = total.astype(BF)


def backward_product(d_full, own_weight, other_weight):
    piece, width = d_full.shape[1:]
    return pl.pallas_call(
        backward_kernel,
        out_shape=jax.ShapeDtypeStruct((NX, NY * piece, own_weight.shape[0] // NX), BF),
        compiler_params=params(),
        name="backward_product",
    )(d_full, own_weight, other_weight)


def weight_kernel(x_ref, d_ref, own_ref, other_ref, own_bias_ref, other_bias_ref):
    parts, rows, width = x_ref.shape
    dims = (((0,), (0,)), ((), ()))
    for u, (out_ref, bias_ref) in enumerate(((other_ref, other_bias_ref), (own_ref, own_bias_ref))):
        delta = rows_of(d_ref, 1 - u)
        for part in range(parts):
            out_ref[part * width : (part + 1) * width, :] = lax.dot_general(
                x_ref[part], delta, dims, preferred_element_type=F32
            )
        total = jnp.sum(delta.astype(F32), axis=0, keepdims=True)
        bias_ref[...] = jnp.broadcast_to(total, bias_ref.shape)


def weight_product(x_full, d_full):
    parts, rows, width = x_full.shape
    out = jax.ShapeDtypeStruct((parts * width, d_full.shape[2]), F32)
    bias = jax.ShapeDtypeStruct((8, d_full.shape[2]), F32)
    return pl.pallas_call(
        weight_kernel,
        out_shape=[out, out, bias, bias],
        compiler_params=params(),
        name="weight_product",
    )(x_full, d_full)


def table_kernel(counts_ref, g_ref, own_ref, other_ref):
    feats, slots, rows = counts_ref.shape
    half = slots // 2
    for feat in range(feats):
        other_ref[feat] = jnp.dot(counts_ref[feat, half:, :], g_ref[feat], preferred_element_type=F32)
        own_ref[feat] = jnp.dot(counts_ref[feat, :half, :], g_ref[feat], preferred_element_type=F32)


def table_product(counts, grad_full):
    feats, slots, rows = counts.shape
    out = jax.ShapeDtypeStruct((feats, slots // 2, grad_full.shape[2]), F32)
    return pl.pallas_call(
        table_kernel, out_shape=[out, out], compiler_params=params(), name="table_product"
    )(counts, grad_full)


def body(tables, bag_index, cross_weight, cross_bias, upstream):
    feats, shard, width = tables.shape
    layers = cross_weight.shape[0]
    half_rows = bag_index.shape[0] // NS
    s, y, x, z = (lax.axis_index(name) for name in ALL)
    chip = y * NX + x

    other_table = other_core(tables)
    other_weight = other_core(cross_weight)
    g_u = lax.all_to_all(upstream, "x", 1, 0, tiled=True).astype(F32)

    mine = lax.dynamic_slice_in_dim(bag_index, s * half_rows, half_rows, 0)
    mine = jnp.transpose(mine, (1, 2, 0))
    own_id = mine - (s * NY * NX + chip) * shard
    other_id = mine - ((1 - s) * NY * NX + chip) * shard
    own_fits = (own_id >= 0) & (own_id < shard)
    other_fits = (other_id >= 0) & (other_id < shard)
    slot = jnp.where(own_fits, own_id, jnp.where(other_fits, other_id + shard, -1))
    counts, pooled_part = pool(slot.astype(F32), tables, other_table)

    piece_rows = half_rows // NY
    as_pieces = lambda v: v.reshape(NX * NY, piece_rows, width)
    as_parts = lambda v: v.reshape(NX, half_rows, width)
    pooled = scatter_plane(as_pieces(pooled_part)).astype(BF)
    pooled_wide = pooled.astype(F32)
    bias = lax.dynamic_slice(
        cross_bias, (0, z * feats * width + x * width), (layers, width)
    )

    current = pooled
    full_inputs, mixed = [], []
    for layer in range(layers):
        x_full = as_parts(gather_plane(current))
        full_inputs.append(x_full)
        partial = forward_product(x_full, cross_weight[layer], other_weight[layer])
        summed = scatter_depth(partial)
        value = t_to_u(summed.astype(BF)).astype(F32) + bias[layer][None]
        mixed.append(value)
        current = (pooled_wide * value + current.astype(F32)).astype(BF)
    crossed = lax.all_to_all(current, "x", 0, 1, tiled=True)

    carried = jnp.zeros_like(g_u)
    weight_grads, bias_grads = [None] * layers, [None] * layers
    for layer in reversed(range(layers)):
        delta = (pooled_wide * g_u).astype(BF)
        d_full = gather_depth(u_to_t(delta))
        own, other, own_bias, other_bias = weight_product(full_inputs[layer], d_full)
        weight_grads[layer] = own + other_core(other)
        bias_grads[layer] = (own_bias + other_core(other_bias))[0]
        carried = carried + g_u * mixed[layer]
        back = backward_product(d_full, cross_weight[layer], other_weight[layer])
        g_u = g_u + scatter_plane(as_pieces(back))
    total = (g_u + carried).astype(BF)
    grad_full = as_parts(gather_plane(total))
    own, other = table_product(counts, grad_full)
    table_grad = own + other_core(other)
    row_at = y * piece_rows + x * (piece_rows // NX)
    mine = lax.dynamic_slice_in_dim(grad_full, row_at, piece_rows // NX, 1)
    pooled_grad = jnp.transpose(mine, (1, 0, 2)).reshape(piece_rows // NX, NX * width).astype(F32)
    return (crossed, pooled_grad, table_grad, jnp.stack(weight_grads), jnp.stack(bias_grads))


def solution(mesh):
    fine = Mesh(mesh.devices.reshape(NS, NY, NX, NZ), ALL)
    rows = ("s", "y", "x")
    return jax.shard_map(
        body,
        mesh=fine,
        in_specs=(
            P("z", rows, None),
            P(None, "z", None),
            P(None, "z", rows),
            P(),
            P(rows, "z"),
        ),
        out_specs=(
            P(rows, "z"),
            P(rows, "z"),
            P("z", rows, None),
            P(None, "z", rows),
            P(None, rows),
        ),
        check_vma=False,
    )
```

```python
import jax
import jax.numpy as jnp
from jax import lax
from jax.experimental import pallas as pl
from jax.experimental.pallas import tpu as pltpu
from jax.sharding import Mesh, PartitionSpec as P

NS, NY, NX, NZ = 2, 4, 4, 8
ALL = ("s", "y", "x", "z")
BF = jnp.bfloat16
F32 = jnp.float32
VMEM_LIMIT = 16 * 1024 * 1024


def device_number(s, y, x, z):
    return ((s * NY + y) * NX + x) * NZ + z


def pairs_of(target):
    found = []
    for s in range(NS):
        for y in range(NY):
            for x in range(NX):
                for z in range(NZ):
                    found.append((device_number(s, y, x, z), device_number(*target(s, y, x, z))))
    return found


def turned(place, shift):
    return lax.rem(place + shift + NY, NY)


def u_to_t(value):
    return lax.ppermute(
        value, ALL, pairs_of(lambda s, y, x, z: (s, z % NY, x, 2 * y + ((z // NY) ^ s)))
    )


def t_to_u(value):
    return lax.ppermute(
        value, ALL, pairs_of(lambda s, y, x, z: (s, z // 2, x, ((z % 2) ^ s) * NY + y))
    )


def other_core(value):
    return lax.ppermute(value, "s", [(0, 1), (1, 0)])


def scatter_depth(pieces):
    arrived = lax.all_to_all(pieces, "z", 0, 0, tiled=True)
    return jnp.sum(arrived.astype(F32), axis=0)


def gather_depth(piece, *earlier):
    return lax.all_to_all(spread(piece, NZ, *earlier), "z", 0, 0, tiled=True)


def shift_in_y(value, k):
    return lax.ppermute(value, "y", [(i, (i + k) % NY) for i in range(NY)])


def swap_in_x(blocks):
    return lax.all_to_all(blocks, "x", 0, 0, tiled=True)


def gather_in_y(across):
    return [across] + [shift_in_y(across, j) for j in range(1, NY)]


def scatter_in_y(parts):
    return [parts[0]] + [shift_in_y(parts[j], j) for j in range(1, NY)]


def scatter_in_x(parts, *earlier):
    arrived = swap_in_x(add_parts(parts, *earlier))
    return jnp.sum(arrived.astype(F32), axis=0)


def params():
    return pltpu.CompilerParams(vmem_limit_bytes=VMEM_LIMIT)


SCALARS = pl.BlockSpec(memory_space=pltpu.SMEM)
FREE = pl.BlockSpec(memory_space=pl.ANY)


def pool_kernel(at_ref, ids_ref, own_ref, other_ref, counts_ref, *refs):
    pooled_refs, summed_ref = refs[:NY], refs[NY]
    bag_len, rows = ids_ref.shape[1:]
    slots = counts_ref.shape[1]
    lanes = 128
    for first in range(0, rows, lanes):
        slot_ids = lax.broadcasted_iota(jnp.int32, (slots, lanes), 0).astype(F32).astype(BF)
        total = jnp.zeros((slots, lanes), BF)
        for position in range(bag_len):
            wanted = ids_ref[0, position : position + 1, first : first + lanes]
            wanted = jnp.broadcast_to(wanted, (slots, lanes)).astype(BF)
            total = total + jnp.where(wanted == slot_ids, jnp.ones((), BF), jnp.zeros((), BF))
        counts_ref[0, :, first : first + lanes] = total
    half = slots // 2
    dims = (((0,), (0,)), ((), ()))
    summed = lax.dot_general(counts_ref[0, :half, :], own_ref[0], dims, preferred_element_type=F32)
    summed += lax.dot_general(counts_ref[0, half:, :], other_ref[0], dims, preferred_element_type=F32)
    piece = rows // NY
    summed_ref[...] = summed.astype(BF).reshape(NY, piece, summed.shape[1])
    for j in range(NY):
        pooled_refs[j][0] = summed_ref[turned(at_ref[1], j)]


def pool(at, ids, own_table, other_table):
    feats, bag_len, rows = ids.shape
    _, shard, width = own_table.shape
    piece = rows // NY
    one = lambda f: (f, 0, 0)
    return pl.pallas_call(
        pool_kernel,
        grid=(feats,),
        in_specs=[
            SCALARS,
            pl.BlockSpec((1, bag_len, rows), one),
            pl.BlockSpec((1, shard, width), one),
            pl.BlockSpec((1, shard, width), one),
        ],
        out_specs=[pl.BlockSpec((1, 2 * shard, rows), one)] + [pl.BlockSpec((1, piece, width), one)] * NY,
        out_shape=[jax.ShapeDtypeStruct((feats, 2 * shard, rows), BF)]
        + [jax.ShapeDtypeStruct((feats, piece, width), BF)] * NY,
        scratch_shapes=[pltpu.VMEM((NY, piece, width), BF)],
        compiler_params=params(),
        name="pool",
    )(at, ids, own_table, other_table)


def whole(shape):
    return pl.BlockSpec(shape, lambda i: (0,) * len(shape))


def of_layer(weights, layer):
    return pl.BlockSpec((1,) + weights.shape[1:], lambda i: (layer, 0, 0))


def forward_kernel(at_ref, *refs):
    x_refs, w_refs, (out_ref, keep_ref) = refs[:NY], refs[NY : NY + 2], refs[-2:]
    piece, width = x_refs[0].shape[1:]
    places = [turned(at_ref[1], -j) for j in range(NY)]
    totals = [None, None]
    for k in range(NX):
        for x_ref, place in zip(x_refs, places):
            keep_ref[k, pl.ds(pl.multiple_of(place * piece, piece), piece), :] = x_ref[k]
        rows = jnp.concatenate([x_ref[k] for x_ref in x_refs], axis=0)
        for u, w_ref in enumerate(w_refs):
            product = jnp.dot(
                rows, w_ref[0, k * width : (k + 1) * width, :], preferred_element_type=F32
            )
            totals[u] = product if k == 0 else totals[u] + product
    for u, total in enumerate(totals):
        total = total.astype(BF)
        for j, place in enumerate(places):
            out_ref[2 * place + u] = total[j * piece : (j + 1) * piece]


def forward_product(at, x_full, own_weight, other_weight, layer, *earlier):
    parts, piece, width = x_full[0].shape
    out = (NZ, piece, own_weight.shape[2])
    keep = (parts, NY * piece, width)
    return pl.pallas_call(
        forward_kernel,
        grid=(1,),
        in_specs=[SCALARS]
        + [whole(v.shape) for v in x_full]
        + [of_layer(own_weight, layer), of_layer(other_weight, layer)]
        + [FREE] * len(earlier),
        out_specs=[whole(out), whole(keep)],
        out_shape=[jax.ShapeDtypeStruct(out, BF), jax.ShapeDtypeStruct(keep, BF)],
        compiler_params=params(),
        name="forward_product",
    )(at, *x_full, own_weight, other_weight, *earlier)


def backward_kernel(at_ref, d_ref, own_ref, other_ref, keep_ref, *out_refs):
    parts, piece, width = out_refs[0].shape
    dims = (((1,), (1,)), ((), ()))
    for u in range(2):
        for y in range(NY):
            keep_ref[u, y * piece : (y + 1) * piece, :] = d_ref[2 * y + u]
    places = [turned(at_ref[1], j) for j in range(NY)]
    deltas = [jnp.concatenate([d_ref[2 * y + u] for y in places], axis=0) for u in range(2)]
    for k in range(parts):
        total = None
        for delta, w_ref in zip(deltas, (own_ref, other_ref)):
            product = lax.dot_general(
                delta, w_ref[0, k * width : (k + 1) * width, :], dims, preferred_element_type=F32
            )
            total = product if total is None else total + product
        total = total.astype(BF)
        for j in range(NY):
            out_refs[j][k] = total[j * piece : (j + 1) * piece]


def backward_product(at, d_full, own_weight, other_weight, layer):
    piece, width = d_full.shape[1:]
    out = (NX, piece, own_weight.shape[1] // NX)
    keep = (2, NY * piece, width)
    return pl.pallas_call(
        backward_kernel,
        grid=(1,),
        in_specs=[SCALARS, whole(d_full.shape), of_layer(own_weight, layer), of_layer(other_weight, layer)],
        out_specs=[whole(keep)] + [whole(out)] * NY,
        out_shape=[jax.ShapeDtypeStruct(keep, BF)] + [jax.ShapeDtypeStruct(out, BF)] * NY,
        compiler_params=params(),
        name="backward_product",
    )(at, d_full, own_weight, other_weight)


def weight_kernel(x_ref, d_ref, *refs):
    own_ref, other_ref, own_bias_ref, other_bias_ref = refs[-4:]
    dims = (((0,), (0,)), ((), ()))
    for u, out_ref in ((0, own_ref), (1, other_ref)):
        out_ref[...] = lax.dot_general(x_ref[0], d_ref[u], dims, preferred_element_type=F32)

    @pl.when(pl.program_id(0) == 0)
    def _():
        for u, bias_ref in ((0, own_bias_ref), (1, other_bias_ref)):
            total = jnp.sum(d_ref[u].astype(F32), axis=0, keepdims=True)
            bias_ref[...] = jnp.broadcast_to(total, bias_ref.shape)


def weight_product(x_keep, d_keep, *earlier):
    parts, rows, width = x_keep.shape
    columns = d_keep.shape[2]
    out = jax.ShapeDtypeStruct((parts * width, columns), F32)
    bias = jax.ShapeDtypeStruct((8, columns), F32)
    block = pl.BlockSpec((width, columns), lambda i: (i, 0))
    return pl.pallas_call(
        weight_kernel,
        grid=(parts,),
        in_specs=[pl.BlockSpec((1, rows, width), lambda i: (i, 0, 0)), whole(d_keep.shape)]
        + [FREE] * len(earlier),
        out_specs=[block, block, whole(bias.shape), whole(bias.shape)],
        out_shape=[out, out, bias, bias],
        compiler_params=params(),
        name="weight_product",
    )(x_keep, d_keep, *earlier)


def pack_kernel(g_ref, last_ref, out_ref):
    rows = g_ref.shape[0]
    strip = rows // NX
    for k in range(NX):
        out_ref[k, :rows, :] = g_ref[...]
        out_ref[k, rows:, :] = last_ref[k * strip : (k + 1) * strip, :]


def pack(g, last):
    out = (NX, g.shape[0] + g.shape[0] // NX, g.shape[1])
    return pl.pallas_call(
        pack_kernel,
        grid=(1,),
        in_specs=[whole(g.shape), whole(last.shape)],
        out_specs=whole(out),
        out_shape=jax.ShapeDtypeStruct(out, BF),
        compiler_params=params(),
        name="pack",
    )(g, last)


def unpack_kernel(arrived_ref, across_ref, last_rows_ref):
    rows, width = across_ref.shape[1:]
    for k in range(NX):
        across_ref[k] = arrived_ref[k, :rows, :]
        last_rows_ref[:, k * width : (k + 1) * width] = arrived_ref[k, rows:, :]


def unpack(arrived, rows):
    parts, packed, width = arrived.shape
    across, last_rows = (parts, rows, width), (packed - rows, parts * width)
    return pl.pallas_call(
        unpack_kernel,
        grid=(1,),
        in_specs=[whole(arrived.shape)],
        out_specs=[whole(across), whole(last_rows)],
        out_shape=[jax.ShapeDtypeStruct(across, BF), jax.ShapeDtypeStruct(last_rows, BF)],
        compiler_params=params(),
        name="unpack",
    )(arrived)


def add_kernel(*refs):
    total = refs[0][...].astype(F32)
    for ref in refs[1:NY]:
        total = total + ref[...].astype(F32)
    refs[-1][...] = total.astype(BF)


def add_parts(parts, *earlier):
    shape = parts[0].shape
    block = pl.BlockSpec((1,) + shape[1:], lambda i: (i, 0, 0))
    return pl.pallas_call(
        add_kernel,
        grid=(shape[0],),
        in_specs=[block] * len(parts) + [FREE] * len(earlier),
        out_specs=block,
        out_shape=jax.ShapeDtypeStruct(shape, BF),
        compiler_params=params(),
        name="add_parts",
    )(*parts, *earlier)


def spread_kernel(*refs):
    for at in range(refs[-1].shape[0]):
        refs[-1][at] = refs[0][...]


def spread(piece, count, *earlier):
    out = (count,) + piece.shape
    return pl.pallas_call(
        spread_kernel,
        grid=(1,),
        in_specs=[whole(piece.shape)] + [FREE] * len(earlier),
        out_specs=whole(out),
        out_shape=jax.ShapeDtypeStruct(out, piece.dtype),
        compiler_params=params(),
        name="spread",
    )(piece, *earlier)


def table_kernel(at_ref, counts_ref, *refs):
    g_refs, (own_ref, other_ref, rows_ref) = refs[:NY], refs[-3:]
    feats, slots, rows = counts_ref.shape
    piece, width = g_refs[0].shape[1:]
    half = slots // 2
    firsts = [pl.multiple_of(turned(at_ref[1], -j) * piece, piece) for j in range(NY)]

    def step(k, carry):
        grads = jnp.concatenate([g_ref[k] for g_ref in g_refs], axis=0)
        for out_ref, first_slot in ((other_ref, half), (own_ref, 0)):
            counted = jnp.concatenate(
                [counts_ref[k, pl.ds(first_slot, half), pl.ds(first, piece)] for first in firsts],
                axis=1,
            )
            out_ref[k] = jnp.dot(counted, grads, preferred_element_type=F32)
        return carry

    lax.fori_loop(0, feats, step, 0)
    mine = rows_ref.shape[0]
    first = pl.multiple_of(at_ref[0] * mine, mine)
    for k in range(feats):
        rows_ref[:, k * width : (k + 1) * width] = g_refs[0][k, pl.ds(first, mine), :].astype(F32)


def table_product(at, counts, grad_full, *earlier):
    feats, slots, rows = counts.shape
    width = grad_full[0].shape[2]
    out = (feats, slots // 2, width)
    mine = (rows // (NX * NY), feats * width)
    return pl.pallas_call(
        table_kernel,
        grid=(1,),
        in_specs=[SCALARS, whole(counts.shape)]
        + [whole(v.shape) for v in grad_full]
        + [FREE] * len(earlier),
        out_specs=[whole(out), whole(out), whole(mine)],
        out_shape=[jax.ShapeDtypeStruct(v, F32) for v in (out, out, mine)],
        compiler_params=params(),
        name="table_product",
    )(at, counts, *grad_full, *earlier)


def body(tables, bag_index, cross_weight, cross_bias, upstream):
    feats, shard, width = tables.shape
    layers = cross_weight.shape[0]
    half_rows = bag_index.shape[0] // NS
    s, y, x, z = (lax.axis_index(name) for name in ALL)
    chip = y * NX + x
    at = jnp.stack([x, y]).astype(jnp.int32)

    other_table = other_core(tables)
    other_weight = other_core(cross_weight)
    columns = jnp.stack([upstream[:, a * width : (a + 1) * width] for a in range(NX)])
    swapped = swap_in_x(columns)
    g_u = swapped.reshape(-1, width).astype(F32)

    mine = lax.dynamic_slice_in_dim(bag_index, s * half_rows, half_rows, 0)
    mine = jnp.transpose(mine, (1, 2, 0))
    own_id = mine - (s * NY * NX + chip) * shard
    other_id = mine - ((1 - s) * NY * NX + chip) * shard
    own_fits = (own_id >= 0) & (own_id < shard)
    other_fits = (other_id >= 0) & (other_id < shard)
    slot = jnp.where(own_fits, own_id, jnp.where(other_fits, other_id + shard, -1))
    counts, *pooled_parts = pool(at, slot.astype(F32), tables, other_table)

    piece_rows = half_rows // NY
    pooled = scatter_in_x(scatter_in_y(pooled_parts), swapped).astype(BF)
    pooled_wide = pooled.astype(F32)
    bias = lax.dynamic_slice(cross_bias, (0, z * feats * width + x * width), (layers, width))

    current = pooled
    x_keeps, d_keeps = [None] * layers, [None] * layers
    mixed, held_grads = [], [None] * layers
    for step in range(layers):
        layer, back_layer = step, layers - 1 - step
        delta = (pooled_wide * g_u).astype(BF)
        across = swap_in_x(spread(current, NX))
        d_full = gather_depth(u_to_t(delta), *([across] if step == 0 else []))
        x_full = gather_in_y(across)
        partial, x_keep = forward_product(at, x_full, cross_weight, other_weight, layer)
        d_keep, *back = backward_product(at, d_full, cross_weight, other_weight, back_layer)
        back = scatter_in_y(back)
        x_keeps[layer], d_keeps[back_layer] = x_keep, d_keep
        summed = scatter_depth(partial).astype(BF)
        held_grads[back_layer] = g_u
        g_u = g_u + scatter_in_x(back)
        value = t_to_u(summed).astype(F32) + bias[layer][None]
        mixed.append(value)
        current = (pooled_wide * value + current.astype(F32)).astype(BF)
    for layer in range(layers):
        g_u = g_u + held_grads[layer] * mixed[layer]
    total = g_u.astype(BF)
    across, crossed = unpack(swap_in_x(pack(total, current)), piece_rows)
    grad_full = gather_in_y(across)
    weight_grads, bias_grads = [None] * layers, [None] * layers
    for layer in reversed(range(layers)):
        own, other, own_bias, other_bias = weight_product(
            x_keeps[layer], d_keeps[layer], back[1]
        )
        weight_grads[layer] = own + other_core(other)
        bias_grads[layer] = (own_bias + other_core(other_bias))[0]
    weight_grad, bias_grad = jnp.stack(weight_grads), jnp.stack(bias_grads)
    own, other, pooled_grad = table_product(at, counts, grad_full, weight_grad, bias_grad)
    table_grad = own + other_core(other)
    return crossed, pooled_grad, table_grad, weight_grad, bias_grad


def solution(mesh):
    fine = Mesh(mesh.devices.reshape(NS, NY, NX, NZ), ALL)
    rows = ("s", "y", "x")
    return jax.shard_map(
        body,
        mesh=fine,
        in_specs=(
            P("z", rows, None),
            P(None, "z", None),
            P(None, "z", rows),
            P(),
            P(rows, "z"),
        ),
        out_specs=(
            P(rows, "z"),
            P(rows, "z"),
            P("z", rows, None),
            P(None, "z", rows),
            P(None, rows),
        ),
        check_vma=False,
    )
```

```python
import jax
import jax.numpy as jnp
from jax import lax
from jax.experimental import pallas as pl
from jax.experimental.pallas import tpu as pltpu
from jax.sharding import Mesh, PartitionSpec as P

NS, NY, NX, NZ = 2, 4, 4, 8
BF = jnp.bfloat16
F32 = jnp.float32
VMEM_LIMIT = 16 * 1024 * 1024
NN = (((1,), (0,)), ((), ()))
NT = (((1,), (1,)), ((), ()))
TN = (((0,), (0,)), ((), ()))


def dot(left, right, dims):
    return lax.dot_general(left, right, dims, preferred_element_type=F32)


def turned(place, shift):
    return lax.rem(place + shift + 4, 4)


def other_core(value):
    return lax.ppermute(value, "s", [(0, 1), (1, 0)])


def shift_in(axis, value, k):
    return lax.ppermute(value, axis, [(i, (i + k) % 4) for i in range(4)])


def swap(axis, pieces):
    return lax.all_to_all(pieces, axis, 0, 0, tiled=True)


SCALARS = pl.BlockSpec(memory_space=pltpu.SMEM)
FREE = pl.BlockSpec(memory_space=pl.ANY)


def whole(shape):
    return pl.BlockSpec(shape, lambda i: (0,) * len(shape))


def call(kernel, ins, outs, earlier=(), name=None):
    specs = [spec if spec is not None else whole(v.shape) for v, spec in ins]
    return pl.pallas_call(
        kernel,
        grid=(1,),
        in_specs=specs + [FREE] * len(earlier),
        out_specs=[whole(v.shape) for v in outs],
        out_shape=outs,
        compiler_params=pltpu.CompilerParams(vmem_limit_bytes=VMEM_LIMIT),
        name=name,
    )(*[v for v, _ in ins], *earlier)


def nothing_kernel(*refs):
    pass


def after(value, *earlier):
    return pl.pallas_call(
        nothing_kernel,
        in_specs=[FREE] * (1 + len(earlier)),
        out_specs=FREE,
        out_shape=like(value.shape, value.dtype),
        input_output_aliases={0: 0},
        name="after",
    )(value, *earlier)


def like(shape, kind=BF):
    return jax.ShapeDtypeStruct(shape, kind)


def count_kernel(ids_ref, counts_ref):
    bag_len, rows = ids_ref.shape[1:]
    slots = counts_ref.shape[1]
    lanes = 128
    for first in range(0, rows, lanes):
        slot_ids = lax.broadcasted_iota(jnp.int32, (slots, lanes), 0).astype(F32).astype(BF)
        total = jnp.zeros((slots, lanes), BF)
        for position in range(bag_len):
            wanted = ids_ref[0, position : position + 1, first : first + lanes]
            wanted = jnp.broadcast_to(wanted, (slots, lanes)).astype(BF)
            total = total + jnp.where(wanted == slot_ids, jnp.ones((), BF), jnp.zeros((), BF))
        counts_ref[0, :, first : first + lanes] = total


def count(ids, slots):
    feats, bag_len, rows = ids.shape
    one = lambda f: (f, 0, 0)
    return pl.pallas_call(
        count_kernel,
        grid=(feats,),
        in_specs=[pl.BlockSpec((1, bag_len, rows), one)],
        out_specs=pl.BlockSpec((1, slots, rows), one),
        out_shape=like((feats, slots, rows)),
        compiler_params=pltpu.CompilerParams(vmem_limit_bytes=VMEM_LIMIT),
        name="count",
    )(ids)


def pool_kernel(at_ref, counts_ref, own_ref, other_ref, *refs):
    feats, slots, rows = counts_ref.shape
    half = slots // 2
    for k, out_ref in enumerate(refs[-feats:]):
        feat = turned(at_ref[0], k)
        summed = dot(own_ref[feat], counts_ref[feat, :half, :], TN)
        summed += dot(other_ref[feat], counts_ref[feat, half:, :], TN)
        out_ref[...] = summed.astype(BF)


def pool(at, counts, own_table, other_table, *earlier):
    feats, _, rows = counts.shape
    return call(
        pool_kernel,
        [(at, SCALARS), (counts, None), (own_table, None), (other_table, None)],
        [like((own_table.shape[2], rows))] * feats,
        earlier,
        "pool",
    )


def forward_kernel(at_ref, *refs):
    x_refs, w_refs, (out_ref, keep_ref) = refs[:NX], refs[NX : NX + 2], refs[-2:]
    width = x_refs[0].shape[0]
    s = at_ref[2]
    for u, w_ref in enumerate(w_refs):
        weight = w_ref[:, 0]
        weight_shape = (weight.shape[0] * weight.shape[1], width)
        total = None
        for k, x_ref in enumerate(x_refs):
            part = turned(at_ref[0], -k)
            block = pl.multiple_of(part * width, width)
            if u == 0:
                keep_ref[part] = x_ref[...]
            weight = w_ref[:, 0, :, pl.ds(block, width)].reshape(weight_shape)
            product = dot(weight, x_ref[...], NN)
            total = product if total is None else total + product
        total = total.astype(BF).reshape((NY, -1, total.shape[1]))
        first = NY * (s if u == 0 else 1 - s)
        for y in range(NY):
            out_ref[first + y] = total[y]


def of_layer(weights, layer):
    parts, layers, rows, columns = weights.shape
    return pl.BlockSpec((parts, 1, rows, columns), lambda i: (0, layer, 0, 0))


def forward_product(at, x_full, own_weight, other_weight, layer, *earlier):
    width, rows = x_full[0].shape
    return call(
        forward_kernel,
        [(at, SCALARS)]
        + [(v, None) for v in x_full]
        + [(v, of_layer(v, layer)) for v in (own_weight, other_weight)],
        [like((NZ, own_weight.shape[2], rows)), like((NX, width, rows))],
        earlier,
        "forward_product",
    )


def backward_kernel(at_ref, d_ref, own_ref, other_ref, *refs):
    out_refs = refs[-NX:]
    width, rows = out_refs[0].shape
    s = at_ref[2]
    firsts = (NY * s, NY * (1 - s))
    deltas = [
        jnp.concatenate([d_ref[first + y] for y in range(NY)], axis=0) for first in firsts
    ]
    for k, out_ref in enumerate(out_refs):
        block = pl.multiple_of(turned(at_ref[0], k) * width, width)
        total = None
        for delta, w_ref in zip(deltas, (own_ref, other_ref)):
            weight = w_ref[:, 0, :, pl.ds(block, width)].reshape((delta.shape[0], width))
            product = dot(weight, delta, TN)
            total = product if total is None else total + product
        out_ref[...] = total.astype(BF)


def backward_product(at, d_full, own_weight, other_weight, layer, *earlier):
    width, rows = own_weight.shape[3] // NX, d_full.shape[2]
    return call(
        backward_kernel,
        [(at, SCALARS), (d_full, None)]
        + [(v, of_layer(v, layer)) for v in (own_weight, other_weight)],
        [like((width, rows))] * NX,
        earlier,
        "backward_product",
    )


def weight_kernel(x_ref, d_ref, *refs):
    own_ref, other_ref, own_bias_ref, other_bias_ref = refs[-4:]
    columns, rows = own_ref.shape[1], x_ref.shape[2]
    deltas = [d_ref[:, 1 + u].reshape((columns, rows)) for u in range(2)]
    for delta, out_ref in zip(deltas, (own_ref, other_ref)):
        out_ref[...] = dot(x_ref[0], delta, NT)

    @pl.when(pl.program_id(0) == 0)
    def _():
        ones = jnp.ones((8, rows), BF)
        for delta, bias_ref in zip(deltas, (own_bias_ref, other_bias_ref)):
            bias_ref[...] = dot(ones, delta, NT)


def weight_product(x_keep, d_parts, *earlier):
    parts, width, rows = x_keep.shape
    columns = NY * d_parts.shape[2]
    out, bias = like((parts * width, columns), F32), like((8, columns), F32)
    block = pl.BlockSpec((width, columns), lambda i: (i, 0))
    return pl.pallas_call(
        weight_kernel,
        grid=(parts,),
        in_specs=[pl.BlockSpec((1, width, rows), lambda i: (i, 0, 0)), whole(d_parts.shape)]
        + [FREE] * len(earlier),
        out_specs=[block, block, whole(bias.shape), whole(bias.shape)],
        out_shape=[out, out, bias, bias],
        compiler_params=pltpu.CompilerParams(vmem_limit_bytes=VMEM_LIMIT),
        name="weight_product",
    )(x_keep, d_parts, *earlier)


def add_with_kernel(at_ref, d_ref, *refs):
    parts, out_ref = refs[:NX], refs[-1]
    total = parts[0][...].astype(F32)
    for ref in parts[1:]:
        total = total + ref[...].astype(F32)
    _, kinds, piece, _ = out_ref.shape
    total = total.astype(BF)
    s = at_ref[2]
    for y in range(NY):
        out_ref[y, 0] = total[y * piece : (y + 1) * piece]
        out_ref[y, 1] = d_ref[NY * s + y]
        out_ref[y, 2] = d_ref[NY * (1 - s) + y]
        if kinds == 4:
            out_ref[y, 3] = refs[NX][...]


def add_with(at, d_full, parts, following, *earlier):
    _, piece, rows = d_full.shape
    ins = [(at, SCALARS), (d_full, None)] + [(v, None) for v in parts + following]
    out = like((NY, 3 + len(following), piece, rows))
    return call(add_with_kernel, ins, [out], earlier, "add_with")[0]


def add_kernel(*refs):
    total = refs[0][...].astype(F32)
    for ref in refs[1:NX]:
        total = total + ref[...].astype(F32)
    refs[-1][...] = total.astype(BF)


def add_parts(parts, *earlier):
    return call(add_kernel, [(v, None) for v in parts], [like(parts[0].shape)], earlier, "add_parts")[0]


def collect_kernel(at_ref, *refs):
    piece = refs[0].shape[0]
    for j in range(NY):
        place = pl.multiple_of(turned(at_ref[1], -j) * piece, piece)
        refs[-1][pl.ds(place, piece), :] = refs[j][...]


def collect(at, pieces):
    piece, rows = pieces[0].shape
    ins = [(at, SCALARS)] + [(v, None) for v in pieces]
    return call(collect_kernel, ins, [like((NY * piece, rows))], name="collect")[0]


def stack_kernel(at_ref, *refs):
    for j in range(NY):
        refs[-1][turned(at_ref[1], -j)] = refs[j][...]


def stack_from(at, pieces):
    ins = [(at, SCALARS)] + [(v, None) for v in pieces]
    return call(stack_kernel, ins, [like((NY,) + pieces[0].shape)], name="stack_from")[0]


def spread_kernel(*refs):
    for at in range(refs[-1].shape[0]):
        refs[-1][at] = refs[0][...]


def spread(piece, count, *earlier):
    return call(spread_kernel, [(piece, None)], [like((count,) + piece.shape)], earlier, "spread")[0]


def pack_kernel(g_ref, last_ref, *refs):
    out_ref = refs[-1]
    rows = g_ref.shape[1]
    strip = rows // NY
    for place in range(NX * NY):
        out_ref[place, :, :rows] = g_ref[...]
        first = (place % NY) * strip
        out_ref[place, :, rows:] = last_ref[:, first : first + strip]


def pack(g, last, *earlier):
    home, rows = g.shape
    out = like((NX * NY, home, rows + rows // NY))
    return call(pack_kernel, [(g, None), (last, None)], [out], earlier, "pack")[0]


def table_kernel(counts_ref, g_ref, *refs):
    own_ref, other_ref = refs[-2:]
    feats, slots, rows = counts_ref.shape
    half = slots // 2
    for feat in range(feats):
        grads = g_ref[feat * NY : (feat + 1) * NY, :, :rows].reshape((-1, rows))
        other_ref[feat] = dot(counts_ref[feat, half:, :], grads, NT)
        own_ref[feat] = dot(counts_ref[feat, :half, :], grads, NT)


def table_product(counts, arrived, *earlier):
    feats, slots, _ = counts.shape
    out = like((feats, slots // 2, NY * arrived.shape[1]), F32)
    return call(table_kernel, [(counts, None), (arrived, None)], [out, out], earlier, "table_product")


def scatter_in_x(parts):
    return [parts[0]] + [shift_in("x", parts[k], k) for k in range(1, NX)]


def scatter_in_y(parts, *earlier):
    summed = add_parts(parts, *earlier)
    arrived = swap("y", summed.reshape((NY, -1, summed.shape[1])))
    return jnp.sum(arrived.astype(F32), axis=0)


def gather_in_y(at, piece):
    return collect(at, [piece] + [shift_in("y", piece, j) for j in range(1, NY)])


def gather_in_x(block):
    return [block] + [shift_in("x", block, k) for k in range(1, NX)]


def body(tables, bag_index, cross_weight, cross_bias, upstream):
    feats, shard, width = tables.shape
    layers, in_width, out_width = cross_weight.shape
    half_rows = bag_index.shape[0] // NS
    my_rows = upstream.shape[0]
    home = width // NY
    s, y, x, z = (lax.axis_index(name) for name in ("s", "y", "x", "z"))
    chip = y * NX + x
    at = jnp.stack([x, y, s]).astype(jnp.int32)

    other_table = other_core(tables)
    turned_weight = jnp.transpose(cross_weight.reshape(layers, in_width, NY, home), (2, 0, 3, 1))
    pick = lambda k: lax.dynamic_index_in_dim(turned_weight, turned(y, k), 0, keepdims=False)
    own_weight = stack_from(at, [pick(0)] + [shift_in("y", pick(k), k) for k in range(1, NY)])
    other_weight = other_core(own_weight)
    sent = jnp.transpose(upstream.reshape(my_rows, NX * NY, home), (1, 0, 2))
    swapped = swap(("x", "y"), sent)
    g = jnp.transpose(swapped.reshape(NX, NY, my_rows, home), (3, 1, 0, 2))
    g = g.reshape(home, half_rows).astype(F32)

    mine = lax.dynamic_slice_in_dim(bag_index, s * half_rows, half_rows, 0)
    mine = jnp.transpose(mine, (1, 2, 0))
    own_id = mine - (s * NY * NX + chip) * shard
    other_id = mine - ((1 - s) * NY * NX + chip) * shard
    own_fits = (own_id >= 0) & (own_id < shard)
    other_fits = (other_id >= 0) & (other_id < shard)
    slot = jnp.where(own_fits, own_id, jnp.where(other_fits, other_id + shard, -1))
    counts = count(slot.astype(F32), 2 * shard)
    pooled_parts = pool(at, counts, tables, other_table)

    pooled = scatter_in_y(scatter_in_x(pooled_parts), own_weight, swapped).astype(BF)
    pooled_wide = pooled.astype(F32)
    bias = lax.dynamic_slice(cross_bias, (0, z * in_width + x * width + y * home), (layers, home))

    current = pooled
    x_keeps, d_parts = [None] * layers, [None] * layers
    mixed, held = [], [None] * layers
    for step in range(layers):
        layer, back_layer = step, layers - 1 - step
        delta = (pooled_wide * g).astype(BF)
        d_full = swap("z", spread(delta, NZ))
        if step == 0:
            block = gather_in_y(at, current)
        x_full = gather_in_x(block)
        partial, x_keeps[layer] = forward_product(at, x_full, own_weight, other_weight, layer)
        partial = after(partial, d_full)
        back = backward_product(at, d_full, own_weight, other_weight, back_layer, x_keeps[layer])
        back = scatter_in_x(back)
        held[back_layer] = g
        product = swap("z", partial)
        summed = jnp.sum(product.astype(F32), axis=0)
        mixed.append(summed + bias[layer][:, None])
        current = (pooled_wide * mixed[layer] + current.astype(F32)).astype(BF)
        if step < layers - 1:
            sent = add_with(at, d_full, back, [current])
        else:
            late_grads = weight_product(x_keeps[layer], d_parts[layer], back[1])
            sent = add_with(at, d_full, back, [], product, late_grads[0])
        d_parts[back_layer] = swap("y", sent)
        g = g + jnp.sum(d_parts[back_layer][:, 0].astype(F32), axis=0)
        if step < layers - 1:
            block = d_parts[back_layer][:, 3].reshape(width, half_rows)
    for layer in range(layers):
        g = g + held[layer] * mixed[layer]
    packed = pack(g.astype(BF), current)
    arrived = swap(("x", "y"), packed)

    weight_grads, bias_grads = [None] * layers, [None] * layers
    for layer in reversed(range(layers)):
        if layer == layers - 1:
            own, other, own_bias, other_bias = late_grads
        else:
            own, other, own_bias, other_bias = weight_product(x_keeps[layer], d_parts[layer], packed)
        weight_grads[layer] = own + other_core(other)
        bias_grads[layer] = (own_bias + other_core(other_bias))[0]
    weight_grad, bias_grad = jnp.stack(weight_grads), jnp.stack(bias_grads)
    own, other = table_product(counts, arrived)
    table_grad = own + other_core(other)

    strip = half_rows // NY

    def my_part(first):
        part = lax.dynamic_slice(arrived, (0, 0, first), (NX * NY, home, my_rows))
        return jnp.transpose(part, (2, 0, 1)).reshape(my_rows, in_width)

    crossed = my_part(half_rows + x * my_rows)
    pooled_grad = my_part(y * strip + x * my_rows).astype(F32)
    return crossed, pooled_grad, table_grad, weight_grad, bias_grad


def solution(mesh):
    fine = Mesh(mesh.devices.reshape(NS, NY, NX, NZ), ("s", "y", "x", "z"))
    rows = ("s", "y", "x")
    return jax.shard_map(
        body,
        mesh=fine,
        in_specs=(
            P("z", rows, None),
            P(None, "z", None),
            P(None, "z", rows),
            P(),
            P(rows, "z"),
        ),
        out_specs=(
            P(rows, "z"),
            P(rows, "z"),
            P("z", rows, None),
            P(None, "z", rows),
            P(None, rows),
        ),
        check_vma=False,
    )
```

```python
import jax
import jax.numpy as jnp
from jax import lax
from jax.experimental import pallas as pl
from jax.experimental.pallas import tpu as pltpu
from jax.sharding import Mesh, PartitionSpec as P

NS, NY, NX, NZ = 2, 4, 4, 8
BF = jnp.bfloat16
F32 = jnp.float32
VMEM_LIMIT = 16 * 1024 * 1024
NN = (((1,), (0,)), ((), ()))
NT = (((1,), (1,)), ((), ()))
TN = (((0,), (0,)), ((), ()))


def dot(left, right, dims):
    return lax.dot_general(left, right, dims, preferred_element_type=F32)


def turned(place, shift):
    return lax.rem(place + shift + 4, 4)


def other_core(value):
    return lax.ppermute(value, "s", [(0, 1), (1, 0)])


def shift_in(axis, value, k):
    return lax.ppermute(value, axis, [(i, (i + k) % 4) for i in range(4)])


def swap(axis, pieces):
    return lax.all_to_all(pieces, axis, 0, 0, tiled=True)


SCALARS = pl.BlockSpec(memory_space=pltpu.SMEM)
FREE = pl.BlockSpec(memory_space=pl.ANY)


def whole(shape):
    return pl.BlockSpec(shape, lambda i: (0,) * len(shape))


def call(kernel, ins, outs, earlier=(), name=None):
    specs = [spec if spec is not None else whole(v.shape) for v, spec in ins]
    return pl.pallas_call(
        kernel,
        grid=(1,),
        in_specs=specs + [FREE] * len(earlier),
        out_specs=[whole(v.shape) for v in outs],
        out_shape=outs,
        compiler_params=pltpu.CompilerParams(vmem_limit_bytes=VMEM_LIMIT),
        name=name,
    )(*[v for v, _ in ins], *earlier)


def nothing_kernel(*refs):
    pass


def after(value, *earlier):
    return pl.pallas_call(
        nothing_kernel,
        in_specs=[FREE] * (1 + len(earlier)),
        out_specs=FREE,
        out_shape=like(value.shape, value.dtype),
        input_output_aliases={0: 0},
        name="after",
    )(value, *earlier)


def like(shape, kind=BF):
    return jax.ShapeDtypeStruct(shape, kind)


def count_kernel(ids_ref, counts_ref):
    bag_len, rows = ids_ref.shape[1:]
    slots = counts_ref.shape[1]
    lanes = 128
    for first in range(0, rows, lanes):
        slot_ids = lax.broadcasted_iota(jnp.int32, (slots, lanes), 0).astype(F32).astype(BF)
        total = jnp.zeros((slots, lanes), BF)
        for position in range(bag_len):
            wanted = ids_ref[0, position : position + 1, first : first + lanes]
            wanted = jnp.broadcast_to(wanted, (slots, lanes)).astype(BF)
            total = total + jnp.where(wanted == slot_ids, jnp.ones((), BF), jnp.zeros((), BF))
        counts_ref[0, :, first : first + lanes] = total


def count(ids, slots):
    feats, bag_len, rows = ids.shape
    one = lambda f: (f, 0, 0)
    return pl.pallas_call(
        count_kernel,
        grid=(feats,),
        in_specs=[pl.BlockSpec((1, bag_len, rows), one)],
        out_specs=pl.BlockSpec((1, slots, rows), one),
        out_shape=like((feats, slots, rows)),
        compiler_params=pltpu.CompilerParams(vmem_limit_bytes=VMEM_LIMIT),
        name="count",
    )(ids)


def pool_kernel(at_ref, counts_ref, own_ref, other_ref, *refs):
    feats, slots, rows = counts_ref.shape
    half = slots // 2
    for k, out_ref in enumerate(refs[-feats:]):
        feat = turned(at_ref[0], k)
        summed = dot(own_ref[feat], counts_ref[feat, :half, :], TN)
        summed += dot(other_ref[feat], counts_ref[feat, half:, :], TN)
        out_ref[...] = summed.astype(BF)


def pool(at, counts, own_table, other_table, *earlier):
    feats, _, rows = counts.shape
    return call(
        pool_kernel,
        [(at, SCALARS), (counts, None), (own_table, None), (other_table, None)],
        [like((own_table.shape[2], rows))] * feats,
        earlier,
        "pool",
    )


def forward_kernel(at_ref, *refs):
    x_refs, w_refs, (out_ref, keep_ref) = refs[:NX], refs[NX : NX + 2], refs[-2:]
    width = x_refs[0].shape[0]
    s = at_ref[2]
    for u, w_ref in enumerate(w_refs):
        weight = w_ref[:, 0]
        weight_shape = (weight.shape[0] * weight.shape[1], width)
        total = None
        for k, x_ref in enumerate(x_refs):
            part = turned(at_ref[0], -k)
            block = pl.multiple_of(part * width, width)
            if u == 0:
                keep_ref[part] = x_ref[...]
            weight = w_ref[:, 0, :, pl.ds(block, width)].reshape(weight_shape)
            product = dot(weight, x_ref[...], NN)
            total = product if total is None else total + product
        total = total.astype(BF).reshape((NY, -1, total.shape[1]))
        first = NY * (s if u == 0 else 1 - s)
        for y in range(NY):
            out_ref[first + y] = total[y]


def of_layer(weights, layer):
    parts, layers, rows, columns = weights.shape
    return pl.BlockSpec((parts, 1, rows, columns), lambda i: (0, layer, 0, 0))


def forward_product(at, x_full, own_weight, other_weight, layer, *earlier):
    width, rows = x_full[0].shape
    return call(
        forward_kernel,
        [(at, SCALARS)]
        + [(v, None) for v in x_full]
        + [(v, of_layer(v, layer)) for v in (own_weight, other_weight)],
        [like((NZ, own_weight.shape[2], rows)), like((NX, width, rows))],
        earlier,
        "forward_product",
    )


def backward_kernel(at_ref, d_ref, own_ref, other_ref, *refs):
    out_refs = refs[-NX:]
    width, rows = out_refs[0].shape
    s = at_ref[2]
    firsts = (NY * s, NY * (1 - s))
    deltas = [
        jnp.concatenate([d_ref[first + y] for y in range(NY)], axis=0) for first in firsts
    ]
    for k, out_ref in enumerate(out_refs):
        block = pl.multiple_of(turned(at_ref[0], k) * width, width)
        total = None
        for delta, w_ref in zip(deltas, (own_ref, other_ref)):
            weight = w_ref[:, 0, :, pl.ds(block, width)].reshape((delta.shape[0], width))
            product = dot(weight, delta, TN)
            total = product if total is None else total + product
        out_ref[...] = total.astype(BF)


def backward_product(at, d_full, own_weight, other_weight, layer, *earlier):
    width, rows = own_weight.shape[3] // NX, d_full.shape[2]
    return call(
        backward_kernel,
        [(at, SCALARS), (d_full, None)]
        + [(v, of_layer(v, layer)) for v in (own_weight, other_weight)],
        [like((width, rows))] * NX,
        earlier,
        "backward_product",
    )


def weight_kernel(x_ref, d_ref, *refs):
    own_ref, other_ref, own_bias_ref, other_bias_ref = refs[-4:]
    columns, rows = own_ref.shape[1], x_ref.shape[2]
    deltas = [d_ref[:, 1 + u].reshape((columns, rows)) for u in range(2)]
    for delta, out_ref in zip(deltas, (own_ref, other_ref)):
        out_ref[...] = dot(x_ref[0], delta, NT)

    @pl.when(pl.program_id(0) == 0)
    def _():
        ones = jnp.ones((8, rows), BF)
        for delta, bias_ref in zip(deltas, (own_bias_ref, other_bias_ref)):
            bias_ref[...] = dot(ones, delta, NT)


def weight_product(x_keep, d_parts, *earlier):
    parts, width, rows = x_keep.shape
    columns = NY * d_parts.shape[2]
    out, bias = like((parts * width, columns), F32), like((8, columns), F32)
    block = pl.BlockSpec((width, columns), lambda i: (i, 0))
    return pl.pallas_call(
        weight_kernel,
        grid=(parts,),
        in_specs=[pl.BlockSpec((1, width, rows), lambda i: (i, 0, 0)), whole(d_parts.shape)]
        + [FREE] * len(earlier),
        out_specs=[block, block, whole(bias.shape), whole(bias.shape)],
        out_shape=[out, out, bias, bias],
        compiler_params=pltpu.CompilerParams(vmem_limit_bytes=VMEM_LIMIT),
        name="weight_product",
    )(x_keep, d_parts, *earlier)


def join_kernel(own_ref, other_ref, *refs):
    refs[-1][0] = own_ref[...] + other_ref[...]


def join(own, other, layer, layers, held=None):
    out = like((layers,) + own.shape, F32)
    place = pl.BlockSpec((1,) + own.shape, lambda i: (layer, 0, 0))
    extra = [] if held is None else [held]
    return pl.pallas_call(
        join_kernel,
        grid=(1,),
        in_specs=[whole(own.shape)] * 2 + [FREE] * len(extra),
        out_specs=place,
        out_shape=out,
        input_output_aliases={2: 0} if extra else {},
        compiler_params=pltpu.CompilerParams(vmem_limit_bytes=VMEM_LIMIT),
        name="join",
    )(own, other, *extra)


def add_with_kernel(at_ref, d_ref, *refs):
    parts, out_ref = refs[:NX], refs[-1]
    total = parts[0][...].astype(F32)
    for ref in parts[1:]:
        total = total + ref[...].astype(F32)
    _, kinds, piece, _ = out_ref.shape
    total = total.astype(BF)
    s = at_ref[2]
    for y in range(NY):
        out_ref[y, 0] = total[y * piece : (y + 1) * piece]
        out_ref[y, 1] = d_ref[NY * s + y]
        out_ref[y, 2] = d_ref[NY * (1 - s) + y]
        if kinds == 4:
            out_ref[y, 3] = refs[NX][...]


def add_with(at, d_full, parts, following, *earlier):
    _, piece, rows = d_full.shape
    ins = [(at, SCALARS), (d_full, None)] + [(v, None) for v in parts + following]
    out = like((NY, 3 + len(following), piece, rows))
    return call(add_with_kernel, ins, [out], earlier, "add_with")[0]


def add_kernel(*refs):
    total = refs[0][...].astype(F32)
    for ref in refs[1:NX]:
        total = total + ref[...].astype(F32)
    refs[-1][...] = total.astype(BF)


def add_parts(parts, *earlier):
    return call(add_kernel, [(v, None) for v in parts], [like(parts[0].shape)], earlier, "add_parts")[0]


def collect_kernel(at_ref, *refs):
    piece = refs[0].shape[0]
    for j in range(NY):
        place = pl.multiple_of(turned(at_ref[1], -j) * piece, piece)
        refs[-1][pl.ds(place, piece), :] = refs[j][...]


def collect(at, pieces):
    piece, rows = pieces[0].shape
    ins = [(at, SCALARS)] + [(v, None) for v in pieces]
    return call(collect_kernel, ins, [like((NY * piece, rows))], name="collect")[0]


def stack_kernel(at_ref, *refs):
    for j in range(NY):
        refs[-1][turned(at_ref[1], -j)] = refs[j][...]


def stack_from(at, pieces):
    ins = [(at, SCALARS)] + [(v, None) for v in pieces]
    return call(stack_kernel, ins, [like((NY,) + pieces[0].shape)], name="stack_from")[0]


def spread_kernel(*refs):
    for at in range(refs[-1].shape[0]):
        refs[-1][at] = refs[0][...]


def spread(piece, count, *earlier):
    return call(spread_kernel, [(piece, None)], [like((count,) + piece.shape)], earlier, "spread")[0]


def pack_kernel(g_ref, last_ref, *refs):
    out_ref = refs[-1]
    rows = g_ref.shape[1]
    strip = rows // NY
    for place in range(NX * NY):
        out_ref[place, :, :rows] = g_ref[...]
        first = (place % NY) * strip
        out_ref[place, :, rows:] = last_ref[:, first : first + strip]


def pack(g, last, *earlier):
    home, rows = g.shape
    out = like((NX * NY, home, rows + rows // NY))
    return call(pack_kernel, [(g, None), (last, None)], [out], earlier, "pack")[0]


def table_kernel(counts_ref, g_ref, *refs):
    own_ref, other_ref = refs[-2:]
    feats, slots, rows = counts_ref.shape
    half = slots // 2
    for feat in range(feats):
        grads = g_ref[feat * NY : (feat + 1) * NY, :, :rows].reshape((-1, rows))
        other_ref[feat] = dot(counts_ref[feat, half:, :], grads, NT)
        own_ref[feat] = dot(counts_ref[feat, :half, :], grads, NT)


def table_product(counts, arrived, *earlier):
    feats, slots, _ = counts.shape
    out = like((feats, slots // 2, NY * arrived.shape[1]), F32)
    return call(table_kernel, [(counts, None), (arrived, None)], [out, out], earlier, "table_product")


def scatter_in_x(parts):
    return [parts[0]] + [shift_in("x", parts[k], k) for k in range(1, NX)]


def scatter_in_y(parts, *earlier):
    summed = add_parts(parts, *earlier)
    arrived = swap("y", summed.reshape((NY, -1, summed.shape[1])))
    return jnp.sum(arrived.astype(F32), axis=0)


def gather_in_y(at, piece):
    return collect(at, [piece] + [shift_in("y", piece, j) for j in range(1, NY)])


def gather_in_x(block):
    return [block] + [shift_in("x", block, k) for k in range(1, NX)]


def body(tables, bag_index, cross_weight, cross_bias, upstream):
    feats, shard, width = tables.shape
    layers, in_width, out_width = cross_weight.shape
    half_rows = bag_index.shape[0] // NS
    my_rows = upstream.shape[0]
    home = width // NY
    s, y, x, z = (lax.axis_index(name) for name in ("s", "y", "x", "z"))
    chip = y * NX + x
    at = jnp.stack([x, y, s]).astype(jnp.int32)

    other_table = other_core(tables)
    turned_weight = jnp.transpose(cross_weight.reshape(layers, in_width, NY, home), (2, 0, 3, 1))
    pick = lambda k: lax.dynamic_index_in_dim(turned_weight, turned(y, k), 0, keepdims=False)
    own_weight = stack_from(at, [pick(0)] + [shift_in("y", pick(k), k) for k in range(1, NY)])
    other_weight = other_core(own_weight)
    sent = jnp.transpose(upstream.reshape(my_rows, NX * NY, home), (1, 0, 2))
    swapped = swap(("x", "y"), sent)
    g = jnp.transpose(swapped.reshape(NX, NY, my_rows, home), (3, 1, 0, 2))
    g = g.reshape(home, half_rows).astype(F32)

    mine = lax.dynamic_slice_in_dim(bag_index, s * half_rows, half_rows, 0)
    mine = jnp.transpose(mine, (1, 2, 0))
    own_id = mine - (s * NY * NX + chip) * shard
    other_id = mine - ((1 - s) * NY * NX + chip) * shard
    own_fits = (own_id >= 0) & (own_id < shard)
    other_fits = (other_id >= 0) & (other_id < shard)
    slot = jnp.where(own_fits, own_id, jnp.where(other_fits, other_id + shard, -1))
    counts = count(slot.astype(F32), 2 * shard)
    pooled_parts = pool(at, counts, tables, other_table)

    pooled = scatter_in_y(scatter_in_x(pooled_parts), own_weight, swapped).astype(BF)
    pooled_wide = pooled.astype(F32)
    bias = lax.dynamic_slice(cross_bias, (0, z * in_width + x * width + y * home), (layers, home))

    current = pooled
    x_keeps, d_parts = [None] * layers, [None] * layers
    mixed, held = [], [None] * layers
    for step in range(layers):
        layer, back_layer = step, layers - 1 - step
        delta = (pooled_wide * g).astype(BF)
        d_full = swap("z", spread(delta, NZ))
        if step == 0:
            block = gather_in_y(at, current)
        x_full = gather_in_x(block)
        partial, x_keeps[layer] = forward_product(at, x_full, own_weight, other_weight, layer)
        partial = after(partial, d_full)
        back = backward_product(at, d_full, own_weight, other_weight, back_layer, partial)
        back = scatter_in_x(back)
        held[back_layer] = g
        product = swap("z", partial)
        summed = jnp.sum(product.astype(F32), axis=0)
        mixed.append(summed + bias[layer][:, None])
        current = (pooled_wide * mixed[layer] + current.astype(F32)).astype(BF)
        if step < layers - 1:
            sent = add_with(at, d_full, back, [current])
        else:
            late_grads = weight_product(x_keeps[layer], d_parts[layer], back[1])
            sent = add_with(at, d_full, back, [], product, late_grads[0])
        d_parts[back_layer] = swap("y", sent)
        g = g + jnp.sum(d_parts[back_layer][:, 0].astype(F32), axis=0)
        if step < layers - 1:
            block = d_parts[back_layer][:, 3].reshape(width, half_rows)
    for layer in range(layers):
        g = g + held[layer] * mixed[layer]
    packed = pack(g.astype(BF), current)
    arrived = swap(("x", "y"), packed)

    weight_grad, bias_grads = None, [None] * layers
    for layer in reversed(range(layers)):
        if layer == layers - 1:
            own, other, own_bias, other_bias = late_grads
        else:
            own, other, own_bias, other_bias = weight_product(x_keeps[layer], d_parts[layer], packed)
        weight_grad = join(own, other_core(other), layer, layers, weight_grad)
        bias_grads[layer] = (own_bias + other_core(other_bias))[0]
    bias_grad = jnp.stack(bias_grads)
    own, other = table_product(counts, arrived)
    table_grad = own + other_core(other)

    strip = half_rows // NY

    def my_part(first):
        part = lax.dynamic_slice(arrived, (0, 0, first), (NX * NY, home, my_rows))
        return jnp.transpose(part, (2, 0, 1)).reshape(my_rows, in_width)

    crossed = my_part(half_rows + x * my_rows)
    pooled_grad = my_part(y * strip + x * my_rows).astype(F32)
    return crossed, pooled_grad, table_grad, weight_grad, bias_grad


def solution(mesh):
    fine = Mesh(mesh.devices.reshape(NS, NY, NX, NZ), ("s", "y", "x", "z"))
    rows = ("s", "y", "x")
    return jax.shard_map(
        body,
        mesh=fine,
        in_specs=(
            P("z", rows, None),
            P(None, "z", None),
            P(None, "z", rows),
            P(),
            P(rows, "z"),
        ),
        out_specs=(
            P(rows, "z"),
            P(rows, "z"),
            P("z", rows, None),
            P(None, "z", rows),
            P(None, rows),
        ),
        check_vma=False,
    )
```
